256 devices in a mesh: aux: 2 (over core), row: 16 (over x, z_lo), col: 8 (over z_hi, y).
Axes of the slice: x: 4, y: 4, z: 8 (z_hi: 2, z_lo: 4; z = z_hi * 4 + z_lo), core: 2. Of those that a mesh axis runs over, the one named last changes fastest.
Arguments:
- three_index: float32 [4, 6144, 6144], P('aux', 'row', 'col'), as said below
- occupied: float32 [6144, 800], P('col'), may hold values from -0.078125 to 0.078125
Outputs:
- exchange: float32 [6144, 6144], P('row', ('col', 'aux'))
The draws below stay inside these ranges and needn't reach their ends.
Inputs may be any that keep to these rules, and one draw needn't show every extreme that they name: three_index[P, m, l] equals three_index[P, l, m].
All inputs are finite; a program needn't handle non-finite values.
Results may differ from the reference program's by a relative error of at most 0.000065.
Values sent between devices are 32-bit elements; how exact they have to be, the bound alone decides.
No kernel may reach another device: no remote copies, remote signals or barrier semaphores. Data moves between devices by JAX's collectives and lax.ppermute only.
A program may use at most 64 MiB of HBM per device.

```python
import jax
import jax.numpy as jnp
from jax import lax

NBF = 6144
NOCC = 800
NAUX = 4


def draw_three_index(key, part):
    key = jax.random.fold_in(key, 7)
    first = jax.random.fold_in(key, 0)
    factor = (4.0 * NAUX * NOCC) ** (-0.25)
    base = jax.random.normal(first, (NAUX, NBF, NBF), jnp.float32)
    return ((base + jnp.swapaxes(base, 1, 2)) * factor).astype(jnp.float32)


def steps_of(stream_key, dims, cuts, least, largest):
    gain = 1.0
    for dim, shards_of in cuts:
        heights = jax.random.uniform(jax.random.fold_in(jax.random.fold_in(stream_key, 6), dim), (shards_of,), jnp.float32, least / len(cuts), largest / len(cuts))
        gain = gain * jnp.repeat(jnp.exp(heights), dims[dim] // shards_of).reshape((-1,) + (1,) * (len(dims) - 1 - dim))
    return gain


def bell_draw(stream_key, dims, spread, bound, cuts=(), held_as=jnp.bfloat16):
    result = spread * jax.random.normal(stream_key, dims, jnp.float32)
    if cuts:
        result = result * steps_of(stream_key, dims, cuts, -0.22, 0.18)
    return jnp.clip(result, -bound, bound).astype(held_as)


def setup_inputs(seed: int = 0) -> dict:
    splits = jax.random.split(jax.random.key(seed), 3)
    three_index = draw_three_index(jax.random.fold_in(splits[2], 71), 0)
    occupied = bell_draw(splits[1], (NBF, NOCC), NBF ** -0.5, 0.078125, ((0, 8),), jnp.float32)
    return {"three_index": three_index, "occupied": occupied}


def reference(three_index, occupied):
    highest = lax.Precision.HIGHEST
    half = jnp.einsum("pml,li->pmi", three_index, occupied, precision=highest)
    return jnp.einsum("pmi,pni->mn", half, half, precision=highest)
```

```python
import jax
import jax.numpy as jnp
from jax import lax
from jax.sharding import Mesh, PartitionSpec as P

HIGH = lax.Precision.HIGH


def swapped(value, axis):
    return lax.ppermute(value, axis, [(0, 1), (1, 0)])


def shifted(value, axis, distance):
    size = lax.axis_size(axis)
    return lax.ppermute(value, axis, [(i, (i + distance) % size) for i in range(size)])


def body(three_index, occupied):
    aux_here, rows, cols = three_index.shape
    nocc = occupied.shape[1]
    x_size, y_size = lax.axis_size("x"), lax.axis_size("y")
    zl, zh, y = lax.axis_index("zl"), lax.axis_index("zh"), lax.axis_index("y")

    parts = y_size // aux_here
    group = nocc // (parts * x_size)
    padded = -(-group // 8) * 8
    coeff = occupied.reshape(cols, parts * x_size, group)
    coeff = jnp.pad(coeff, ((0, 0), (0, 0), (0, padded - group)))
    coeff = coeff.reshape(cols, parts * x_size * padded)

    half = jnp.einsum("li,pml->pim", coeff, three_index, precision=HIGH)
    half = half.reshape(y_size, x_size, padded, rows)
    half = lax.all_to_all(half, "y", 0, 0, tiled=True)
    part = jnp.sum(half, axis=0)
    part = part + swapped(part, "zh")
    part = lax.all_to_all(part, "x", 0, 0, tiled=True)
    gathered = jnp.stack([part] + [shifted(part, "y", d) for d in (1, 2, 3)])
    mine = lax.dynamic_index_in_dim(gathered, 2 * zh + y // 2, 1, keepdims=False)
    pairs = []
    for yy in range(4):
        for j in range(2):
            source, target = 2 * (yy % 2) + j, 2 * (1 - yy % 2) + j
            pairs.append((source * 4 + yy, target * 4 + yy))
    crossed = lax.ppermute(mine, ("zl", "y"), pairs)
    mine = jnp.where(zl // 2 == y % 2, mine, crossed)
    other = lax.ppermute(mine, "zl", [(0, 1), (1, 0), (2, 3), (3, 2)])
    low = jnp.where(zl % 2 == 0, mine, other)
    high = jnp.where(zl % 2 == 0, other, mine)
    column = jnp.concatenate([low, high], axis=-1)

    tile = jnp.einsum("yxkm,ykn->xmn", gathered, column, precision=HIGH)
    aux = lax.axis_index("aux")
    cut = tile.shape[-1] // 2
    keep = lax.dynamic_slice_in_dim(tile, aux * cut, cut, 2)
    give = lax.dynamic_slice_in_dim(tile, (1 - aux) * cut, cut, 2)
    tile = keep + swapped(give, "aux")
    tile = lax.all_to_all(tile, "x", 0, 0, tiled=True)
    return jnp.sum(tile, axis=0)


def solution(mesh):
    fine = Mesh(mesh.devices.reshape(2, 4, 4, 2, 4), ("aux", "x", "zl", "zh", "y"))
    in_specs = (P("aux", ("x", "zl"), ("zh", "y")), P(("zh", "y"), None))
    out_specs = P(("x", "zl"), ("zh", "y", "aux"))
    return jax.shard_map(body, mesh=fine, in_specs=in_specs, out_specs=out_specs, check_vma=False)
```

```python
import jax
import jax.numpy as jnp
from jax import lax
from jax.sharding import Mesh, PartitionSpec as P

HIGH = lax.Precision.HIGH
CHUNK = 128
SPLIT = (104, 96, 104, 96)


def swapped(value, axis):
    return lax.ppermute(value, axis, [(0, 1), (1, 0)])


def shifted(value, axis, distance):
    size = lax.axis_size(axis)
    return lax.ppermute(value, axis, [(i, (i + distance) % size) for i in range(size)])


def sum_scattered(pieces, axis):
    here = lax.axis_index(axis)
    size = lax.axis_size(axis)
    total = lax.dynamic_index_in_dim(pieces, here, 0, keepdims=False)
    arrived = []
    for d in (2, 1, 3):
        piece = lax.dynamic_index_in_dim(pieces, (here + d) % size, 0, keepdims=False)
        arrived.append(shifted(piece, axis, d))
    return total + arrived[0] + arrived[1] + arrived[2]


def crossing(value):
    pairs = []
    for y in range(4):
        if y % 2 == 0:
            moves = {0: (3, y), 2: (1, y ^ 1)}
        else:
            moves = {3: (0, y), 1: (2, y ^ 1)}
        for z, (to_z, to_y) in moves.items():
            pairs.append((z * 4 + y, to_z * 4 + to_y))
    return lax.ppermute(value, ("zl", "y"), pairs)


def body(three_index, occupied):
    aux_here, rows, cols = three_index.shape
    nocc = occupied.shape[1]
    x_size, y_size = lax.axis_size("x"), lax.axis_size("y")
    aux, zl, zh, y = (lax.axis_index(a) for a in ("aux", "zl", "zh", "y"))
    parts = y_size // aux_here
    padded = max(SPLIT)

    gathered = []
    for start in range(0, rows, CHUNK):
        block = three_index[:, start : start + CHUNK]
        half = jnp.einsum("li,pml->pim", occupied, block, precision=HIGH)
        half = half.reshape(y_size, nocc // parts, CHUNK)
        part = sum_scattered(half, "y")
        part = part + swapped(part, "zh")
        pieces, at = [], 0
        for size in SPLIT:
            pieces.append(jnp.pad(part[at : at + size], ((0, padded - size), (0, 0))))
            at += size
        pieces = jnp.broadcast_to(jnp.stack(pieces)[:, None], (x_size, y_size, padded, CHUNK))
        pieces = pieces.reshape(x_size * y_size, padded, CHUNK)
        pieces = lax.all_to_all(pieces, ("x", "y"), 0, 0, tiled=True)
        gathered.append(pieces.reshape(x_size, y_size * padded, CHUNK))
    left = jnp.concatenate(gathered, axis=-1)

    home = (zl // 2) == (y % 2)
    which = (zl + zl // 2 + y) % 2
    out = []
    for piece in gathered:
        mine = lax.dynamic_index_in_dim(piece, 2 * zh + y // 2, 0, keepdims=False)
        have = jnp.where(home, mine, crossing(mine))
        other = lax.ppermute(have, "zl", [(0, 1), (1, 0), (2, 3), (3, 2)])
        keep = jnp.where(which == aux, have, other)
        give = jnp.where(which == aux, other, have)
        give = jnp.einsum("xkm,kn->xmn", left, give, precision=HIGH)
        keep = jnp.einsum("xkm,kn->xmn", left, keep, precision=HIGH)
        out.append(sum_scattered(keep + swapped(give, "aux"), "x"))
    return jnp.concatenate(out, axis=-1)


def solution(mesh):
    fine = Mesh(mesh.devices.reshape(2, 4, 4, 2, 4), ("aux", "x", "zl", "zh", "y"))
    in_specs = (P("aux", ("x", "zl"), ("zh", "y")), P(("zh", "y"), None))
    out_specs = P(("x", "zl"), ("zh", "y", "aux"))
    return jax.shard_map(body, mesh=fine, in_specs=in_specs, out_specs=out_specs, check_vma=False)
```

```python
import functools

import jax
import jax.numpy as jnp
from jax import lax
from jax.experimental import pallas as pl
from jax.experimental.pallas import tpu as pltpu
from jax.sharding import Mesh, PartitionSpec as P

CHUNK = 128
SPLIT = (104, 96, 104, 96)
PADDED = 104
VMEM_LIMIT = 40 * 1024 * 1024


def halves(value):
    high = value.astype(jnp.bfloat16)
    low = (value - high.astype(jnp.float32)).astype(jnp.bfloat16)
    return high, low


def product(left, right):
    (lh, ll), (rh, rl) = left, right
    dot = functools.partial(jnp.dot, preferred_element_type=jnp.float32)
    return dot(lh, rh) + (dot(lh, rl) + dot(ll, rh))


def call(kernel, out_shape, spaces):
    vmem = pl.BlockSpec(memory_space=pltpu.VMEM)
    smem = pl.BlockSpec(memory_space=pltpu.SMEM)
    return pl.pallas_call(
        kernel,
        out_shape=out_shape,
        in_specs=[smem if s == "s" else vmem for s in spaces],
        out_specs=jax.tree.map(lambda _: vmem, out_shape),
        compiler_params=pltpu.CompilerParams(vmem_limit_bytes=VMEM_LIMIT),
    )


def f32(*shape):
    return jax.ShapeDtypeStruct(shape, jnp.float32)


def bf16(*shape):
    return jax.ShapeDtypeStruct(shape, jnp.bfloat16)


def half_kernel(here_ref, block_ref, coeff_ref, *outs):
    here = here_ref[0]
    coeff = halves(coeff_ref[...])
    size = outs[0].shape[0]
    for p in range(2):
        half = product(halves(block_ref[p]), coeff).T
        for part in range(2):
            piece = half[part * size : (part + 1) * size]
            distance = (2 * p + part - here + 4) % 4
            for d, out in enumerate(outs):

                @pl.when(distance == d)
                def _(out=out, piece=piece):
                    out[...] = piece


def left_kernel(value_ref, high_ref, low_ref):
    for x in range(4):
        high, low = halves(value_ref[x].T)
        high_ref[x] = high
        low_ref[x] = low


def give_kernel(*refs):
    *left, right_ref, out_ref = refs
    right = halves(right_ref[...])
    for c in range(len(left) // 2):
        for x in range(4):
            tile = product((left[2 * c][x], left[2 * c + 1][x]), right)
            out_ref[x, c * CHUNK : (c + 1) * CHUNK] = tile


def keep_kernel(here_ref, *refs):
    left, right_ref, given_ref, outs = refs[:6], refs[6], refs[7], refs[8:]
    here = here_ref[0]
    right = halves(right_ref[...])
    for c in range(len(left) // 2):
        rows = slice(c * CHUNK, (c + 1) * CHUNK)
        for d, out in enumerate(outs):
            x = (here + d) % 4
            tile = product((left[2 * c][x], left[2 * c + 1][x]), right)
            out[rows] = tile + given_ref[x, rows]


def swapped(value, axis):
    return lax.ppermute(value, axis, [(0, 1), (1, 0)])


def shifted(value, axis, distance):
    size = lax.axis_size(axis)
    return lax.ppermute(value, axis, [(i, (i + distance) % size) for i in range(size)])


def tie(value, *others):
    return lax.optimization_barrier((value,) + others)[0]


def crossing(value):
    pairs = []
    for y in range(4):
        if y % 2 == 0:
            moves = {0: (3, y), 2: (1, y ^ 1)}
        else:
            moves = {3: (0, y), 1: (2, y ^ 1)}
        for z, (to_z, to_y) in moves.items():
            pairs.append((z * 4 + y, to_z * 4 + to_y))
    return lax.ppermute(value, ("zl", "y"), pairs)


def body(three_index, occupied):
    aux_here, rows, cols = three_index.shape
    nocc = occupied.shape[1]
    x_size, y_size = lax.axis_size("x"), lax.axis_size("y")
    aux, x, zl, zh, y = (lax.axis_index(a) for a in ("aux", "x", "zl", "zh", "y"))
    share = nocc * aux_here // y_size
    chunks = rows // CHUNK
    x_here, y_here = (a.astype(jnp.int32).reshape(1) for a in (x, y))

    half_call = call(half_kernel, [f32(share, CHUNK)] * 4, "svv")
    left_call = call(left_kernel, [bf16(4, CHUNK, 4 * PADDED)] * 2, "v")
    give_call = call(give_kernel, f32(4, rows, CHUNK), "v" * 7)
    keep_call = call(keep_kernel, [f32(rows, CHUNK)] * 4, "s" + "v" * 8)

    sends = []
    for c in range(chunks):
        block = three_index[:, c * CHUNK : (c + 1) * CHUNK]
        if c:
            block = tie(block, sends[-1][0])
        sends.append(half_call(y_here, block, occupied))

    sums, pieces_of = [], []
    for c in range(chunks):
        own, one, two, three = sends[c]
        if c >= 2:
            two = tie(two, sums[c - 2])
        far = shifted(two, "y", 2)
        if c >= 1:
            one, three = tie(one, sums[c - 1]), tie(three, sums[c - 1])
        total = own + far + shifted(one, "y", 1) + shifted(three, "y", 3)
        sums.append(total)
    gathered = []
    for c in range(chunks):
        part = sums[c] + swapped(sums[c], "zh")
        pieces, at = [], 0
        for size in SPLIT:
            pieces.append(jnp.pad(part[at : at + size], ((0, PADDED - size), (0, 0))))
            at += size
        pieces = jnp.broadcast_to(jnp.stack(pieces)[:, None], (x_size, y_size, PADDED, CHUNK))
        pieces = pieces.reshape(x_size * y_size, PADDED, CHUNK)
        pieces = lax.all_to_all(pieces, ("x", "y"), 0, 0, tiled=True)
        gathered.append(pieces.reshape(x_size, y_size * PADDED, CHUNK))
    left = [a for piece in gathered for a in left_call(piece)]

    home = (zl // 2) == (y % 2)
    which = (zl + zl // 2 + y) % 2
    arrived = []
    for piece in gathered:
        mine = lax.dynamic_index_in_dim(piece, 2 * zh + y // 2, 0, keepdims=False)
        have = jnp.where(home, mine, crossing(mine))
        other = lax.ppermute(have, "zl", [(0, 1), (1, 0), (2, 3), (3, 2)])
        keep = jnp.where(which == aux, have, other)
        give = jnp.where(which == aux, other, have)
        given = swapped(give_call(*left, give), "aux")
        own, one, two, three = keep_call(x_here, *left, keep, given)
        arrived.append((own, shifted(two, "x", 2), shifted(one, "x", 1), shifted(three, "x", 3)))
    return jnp.concatenate([a + b + c + d for a, b, c, d in arrived], axis=-1)


def solution(mesh):
    fine = Mesh(mesh.devices.reshape(2, 4, 4, 2, 4), ("aux", "x", "zl", "zh", "y"))
    in_specs = (P("aux", ("x", "zl"), ("zh", "y")), P(("zh", "y"), None))
    out_specs = P(("x", "zl"), ("zh", "y", "aux"))
    return jax.shard_map(body, mesh=fine, in_specs=in_specs, out_specs=out_specs, check_vma=False)
```

```python
import functools

import jax
import jax.numpy as jnp
from jax import lax
from jax.experimental import pallas as pl
from jax.experimental.pallas import tpu as pltpu
from jax.sharding import Mesh, PartitionSpec as P

CHUNK = 128
SPLIT = (104, 96, 104, 96)
PADDED = 104
DEPTH = 4 * PADDED
VMEM_LIMIT = 32 * 1024 * 1024
HALF_LIMIT = 60 * 1024 * 1024
COST = pl.CostEstimate(flops=int(20e9), bytes_accessed=int(74e6), transcendentals=0)


def halves(value):
    high = value.astype(jnp.bfloat16)
    low = (value - high.astype(jnp.float32)).astype(jnp.bfloat16)
    return high, low


def product(left, right, contract=(1, 0)):
    (lh, ll), (rh, rl) = left, right
    dims = (((contract[0],), (contract[1],)), ((), ()))
    dot = functools.partial(lax.dot_general, dimension_numbers=dims, preferred_element_type=jnp.float32)
    return dot(lh, rh) + (dot(lh, rl) + dot(ll, rh))


def call(kernel, out_shape, spaces, scratch=()):
    vmem = pl.BlockSpec(memory_space=pltpu.VMEM)
    smem = pl.BlockSpec(memory_space=pltpu.SMEM)
    return pl.pallas_call(
        kernel,
        out_shape=out_shape,
        in_specs=[smem if s == "s" else vmem for s in spaces],
        out_specs=jax.tree.map(lambda _: vmem, out_shape),
        scratch_shapes=scratch,
        cost_estimate=COST,
        compiler_params=pltpu.CompilerParams(vmem_limit_bytes=VMEM_LIMIT),
    )


def f32(*shape):
    return jax.ShapeDtypeStruct(shape, jnp.float32)


def bf16(*shape):
    return jax.ShapeDtypeStruct(shape, jnp.bfloat16)


def half_kernel(count, here_ref, coeff_ref, *refs):
    blocks, outs, pieces = refs[:count], refs[count:-1], refs[-1]
    part = pl.program_id(0)
    coeff = halves(coeff_ref[...])
    for c, block in enumerate(blocks):
        for p in range(2):
            pieces[c, 2 * p + part] = product(coeff, halves(block[p]), (1, 1))

    @pl.when(part == 1)
    def _():
        for c in range(count):
            for d in range(4):
                outs[4 * c + d][...] = pieces[c, (here_ref[0] + d) % 4]


def half_call(first, count, here, three_index, coeff):
    size, cols = coeff.shape[0] // 2, coeff.shape[1]
    blocks = [pl.BlockSpec((2, CHUNK, cols), lambda i, c=c: (0, c, 0)) for c in range(first, first + count)]
    return pl.pallas_call(
        functools.partial(half_kernel, count),
        out_shape=[f32(size, CHUNK)] * (4 * count),
        grid=(2,),
        in_specs=[pl.BlockSpec(memory_space=pltpu.SMEM), pl.BlockSpec((size, cols), lambda i: (i, 0))] + blocks,
        out_specs=[pl.BlockSpec((size, CHUNK), lambda i: (0, 0))] * (4 * count),
        scratch_shapes=[pltpu.VMEM((count, 4, size, CHUNK), jnp.float32)],
        cost_estimate=COST,
        compiler_params=pltpu.CompilerParams(vmem_limit_bytes=HALF_LIMIT if first == 0 else VMEM_LIMIT),
    )(here, coeff, *[three_index] * count)


def sum_kernel(a, b, c, d, out):
    out[...] = (a[...] + b[...]) + (c[...] + d[...])


def piece_kernel(one_ref, two_ref, out):
    at = 0
    for i, size in enumerate(SPLIT):
        out[i, :size] = one_ref[at : at + size] + two_ref[at : at + size]
        if size < PADDED:
            out[i, size:] = jnp.zeros((PADDED - size, CHUNK), jnp.float32)
        at += size


def left_kernel(here_ref, pick_ref, a, b, c, d, high_ref, low_ref, mine_ref, held):
    here = here_ref[0]
    for i, ref in enumerate((a, b, c, d)):
        slot = (here - i + 4) % 4
        for e in range(4):
            held[e, slot] = ref[e]
    for e in range(4):
        high, low = halves(held[e].reshape(DEPTH, CHUNK).T)
        high_ref[e] = high
        low_ref[e] = low
    mine_ref[...] = held[pick_ref[0]].reshape(DEPTH, CHUNK)


def have_kernel(flags_ref, mine, crossed, out):
    out[...] = jnp.where(flags_ref[0] == 1, mine[...], crossed[...])


def tile_kernel(flags_ref, *refs):
    left, (have, other), (give_ref, keep_ref) = refs[:6], refs[6:8], refs[8:]
    same = flags_ref[1] == 1
    give = jnp.where(same, other[...], have[...])
    keep = jnp.where(same, have[...], other[...])
    right = halves(jnp.concatenate([give, keep], axis=1))
    for c in range(3):
        rows = slice(c * CHUNK, (c + 1) * CHUNK)
        for e in range(4):
            tile = product((left[2 * c][e], left[2 * c + 1][e]), right)
            give_ref[e, rows] = tile[:, :CHUNK]
            keep_ref[e, rows] = tile[:, CHUNK:]


def add_kernel(here_ref, one_ref, two_ref, *outs):
    for d, out in enumerate(outs):
        x = (here_ref[0] + d) % 4
        out[...] = one_ref[x] + two_ref[x]


def last_kernel(one, two, a, b, c, d, out):
    out[:, :CHUNK] = one[...]
    out[:, CHUNK : 2 * CHUNK] = two[...]
    out[:, 2 * CHUNK :] = (a[...] + b[...]) + (c[...] + d[...])


def swapped(value, axis):
    return lax.ppermute(value, axis, [(0, 1), (1, 0)])


def shifted(value, axis, distance):
    size = lax.axis_size(axis)
    return lax.ppermute(value, axis, [(i, (i + distance) % size) for i in range(size)])


def tie(value, *others):
    return lax.optimization_barrier((value,) + others)[0]


def along(value, moves):
    pairs = [(z * 4 + y, to_z * 4 + to_y) for (z, y), (to_z, to_y) in moves.items()]
    return lax.ppermute(value, ("zl", "y"), pairs)


def crossing(value):
    moves = {}
    for y in range(4):
        if y % 2 == 0:
            moves |= {(0, y): (3, y), (2, y): (1, y ^ 1)}
        else:
            moves |= {(3, y): (0, y), (1, y): (2, y ^ 1)}
    return along(value, moves)


class Order:
    def __init__(self):
        self.last = None

    def __call__(self, kernel, *operands):
        if self.last is not None:
            operands = lax.optimization_barrier(operands + (self.last,))[:-1]
        result = kernel(*operands)
        self.last = result[0] if isinstance(result, (list, tuple)) else result
        return result

    def after(self, value):
        self.last = lax.optimization_barrier((self.last, value))[0]


def body(three_index, occupied):
    rows = three_index.shape[1]
    aux, x, zl, zh, y = (lax.axis_index(a) for a in ("aux", "x", "zl", "zh", "y"))
    home = (zl // 2) == (y % 2)
    same = (zl + zl // 2 + y) % 2 == aux
    scalar = lambda *v: jnp.stack([jnp.asarray(a, jnp.int32) for a in v])
    x_here, y_here = scalar(x), scalar(y)
    pick = scalar(2 * zh + y // 2)
    flags = scalar(home, same)

    coeff = occupied.T
    share = coeff.shape[0] // 2
    sum_call = call(sum_kernel, f32(share, CHUNK), "vvvv")
    piece_call = call(piece_kernel, f32(4, PADDED, CHUNK), "vv")
    left_call = call(
        left_kernel,
        [bf16(4, CHUNK, DEPTH)] * 2 + [f32(DEPTH, CHUNK)],
        "ssvvvv",
        [pltpu.VMEM((4, 4, PADDED, CHUNK), jnp.float32)],
    )
    have_call = call(have_kernel, f32(DEPTH, CHUNK), "svv")
    tile_call = call(tile_kernel, [f32(4, rows, CHUNK)] * 2, "s" + "v" * 8)
    add_call = call(add_kernel, [f32(rows, CHUNK)] * 4, "svv")
    out_call = call(sum_kernel, f32(rows, CHUNK), "vvvv")
    last_call = call(last_kernel, f32(rows, 3 * CHUNK), "v" * 6)

    order = Order()
    first = order(functools.partial(half_call, 0, 1), y_here, three_index, coeff)
    rest = order(functools.partial(half_call, 1, 2), y_here, three_index, coeff)
    sends = [first, rest[:4], rest[4:]]

    def sum_y(c):
        own, one, two, three = sends[c]
        if c == 2:
            one, two, three = lax.optimization_barrier((one, two, three, sums[0][0]))[:3]
        far, near, back = shifted(two, "y", 2), shifted(one, "y", 1), shifted(three, "y", 3)
        total = order(sum_call, own, far, near, back)
        return total, swapped(total, "zh")

    def over_x(total, other):
        return lax.all_to_all(order(piece_call, total, other), "x", 0, 0, tiled=True)

    def over_y(block):
        return [block] + [shifted(block, "y", d) for d in (1, 2, 3)]

    def left_of(blocks):
        high, low, mine = order(left_call, y_here, pick, *blocks)
        return [high, low], mine, crossing(mine)

    def pair_of(mine, crossed):
        have = order(have_call, flags, mine, crossed)
        return have, lax.ppermute(have, "zl", [(0, 1), (1, 0), (2, 3), (3, 2)])

    def tile_of(pair):
        give, keep = order(tile_call, flags, *lefts, *pair)
        return keep, swapped(give, "aux")

    def over_x_sum(keep, given):
        own, one, two, three = order(add_call, x_here, keep, given)
        return [own, shifted(two, "x", 2), shifted(one, "x", 1), shifted(three, "x", 3)]

    sums = []
    for c in range(3):
        sums.append(sum_y(c))
    blocks = []
    for c in range(3):
        block = over_x(*sums[c])
        order.after(block)
        blocks.append(over_y(block))
    left0, mine0, crossed0 = left_of(blocks[0])
    left1, mine1, crossed1 = left_of(blocks[1])
    pair0 = pair_of(mine0, crossed0)
    pair1 = pair_of(mine1, crossed1)
    left2, mine2, crossed2 = left_of(blocks[2])
    lefts = left0 + left1 + left2
    tile0 = tile_of(pair0)
    tile1 = tile_of(pair1)
    pair2 = pair_of(mine2, crossed2)
    out0 = over_x_sum(*tile0)
    out1 = over_x_sum(*tile1)
    tile2 = tile_of(pair2)
    out0 = order(out_call, *out0)
    out2 = over_x_sum(*tile2)
    out1 = order(out_call, *out1)
    return order(last_call, out0, out1, *out2)


def solution(mesh):
    fine = Mesh(mesh.devices.reshape(2, 4, 4, 2, 4), ("aux", "x", "zl", "zh", "y"))
    in_specs = (P("aux", ("x", "zl"), ("zh", "y")), P(("zh", "y"), None))
    out_specs = P(("x", "zl"), ("zh", "y", "aux"))
    return jax.shard_map(body, mesh=fine, in_specs=in_specs, out_specs=out_specs, check_vma=False)
```

```python
import functools

import jax
import jax.numpy as jnp
from jax import lax
from jax.experimental import pallas as pl
from jax.experimental.pallas import tpu as pltpu
from jax.sharding import Mesh, PartitionSpec as P

CHUNK = 128
SPLIT = (104, 96, 104, 96)
PADDED = 104
DEPTH = 4 * PADDED
VMEM_LIMIT = 24 * 1024 * 1024
HALF_LIMIT = 60 * 1024 * 1024
COST = pl.CostEstimate(flops=int(12e9), bytes_accessed=int(44e6), transcendentals=0)


def halves(value):
    high = value.astype(jnp.bfloat16)
    low = (value - high.astype(jnp.float32)).astype(jnp.bfloat16)
    return high, low


def product(left, right, contract=(1, 0)):
    (lh, ll), (rh, rl) = left, right
    dims = (((contract[0],), (contract[1],)), ((), ()))
    dot = functools.partial(lax.dot_general, dimension_numbers=dims, preferred_element_type=jnp.float32)
    return dot(lh, rh) + (dot(lh, rl) + dot(ll, rh))


def call(kernel, out_shape, spaces, scratch=()):
    vmem = pl.BlockSpec(memory_space=pltpu.VMEM)
    smem = pl.BlockSpec(memory_space=pltpu.SMEM)
    return pl.pallas_call(
        kernel,
        out_shape=out_shape,
        in_specs=[smem if s == "s" else vmem for s in spaces],
        out_specs=jax.tree.map(lambda _: vmem, out_shape),
        scratch_shapes=scratch,
        cost_estimate=COST,
        compiler_params=pltpu.CompilerParams(vmem_limit_bytes=VMEM_LIMIT),
    )


def f32(*shape):
    return jax.ShapeDtypeStruct(shape, jnp.float32)


def bf16(*shape):
    return jax.ShapeDtypeStruct(shape, jnp.bfloat16)


def half_kernel(count, here_ref, coeff_ref, *refs):
    blocks, outs, pieces = refs[:count], refs[count:-1], refs[-1]
    part = pl.program_id(0)
    coeff = halves(coeff_ref[...])
    for c, block in enumerate(blocks):
        for p in range(2):
            pieces[c, 2 * p + part] = product(coeff, halves(block[p]), (1, 1))

    @pl.when(part == 1)
    def _():
        for c in range(count):
            for d in range(4):
                outs[4 * c + d][...] = pieces[c, (here_ref[0] + d) % 4]


def half_call(first, count, here, three_index, coeff):
    size, cols = coeff.shape[0] // 2, coeff.shape[1]
    blocks = [pl.BlockSpec((2, CHUNK, cols), lambda i, c=c: (0, c, 0)) for c in range(first, first + count)]
    return pl.pallas_call(
        functools.partial(half_kernel, count),
        out_shape=[f32(size, CHUNK)] * (4 * count),
        grid=(2,),
        in_specs=[pl.BlockSpec(memory_space=pltpu.SMEM), pl.BlockSpec((size, cols), lambda i: (i, 0))] + blocks,
        out_specs=[pl.BlockSpec((size, CHUNK), lambda i: (0, 0))] * (4 * count),
        scratch_shapes=[pltpu.VMEM((count, 4, size, CHUNK), jnp.float32)],
        cost_estimate=COST,
        compiler_params=pltpu.CompilerParams(vmem_limit_bytes=HALF_LIMIT if first == 0 else VMEM_LIMIT),
    )(here, coeff, *[three_index] * count)


def sum_kernel(a, b, c, d, out):
    out[...] = (a[...] + b[...]) + (c[...] + d[...])


def piece_kernel(one_ref, two_ref, out):
    at = 0
    for i, size in enumerate(SPLIT):
        out[i, :size] = one_ref[at : at + size] + two_ref[at : at + size]
        if size < PADDED:
            out[i, size:] = jnp.zeros((PADDED - size, CHUNK), jnp.float32)
        at += size


def left_kernel(here_ref, pick_ref, a, b, c, d, high_ref, low_ref, mine_ref, held):
    here = here_ref[0]
    for i, ref in enumerate((a, b, c, d)):
        slot = (here - i + 4) % 4
        for e in range(4):
            held[e, slot] = ref[e]
    for e in range(4):
        high, low = halves(held[e].reshape(DEPTH, CHUNK).T)
        high_ref[e] = high
        low_ref[e] = low
    mine_ref[...] = held[pick_ref[0]].reshape(DEPTH, CHUNK)


def have_kernel(flags_ref, mine, crossed, out):
    out[...] = jnp.where(flags_ref[0] == 1, mine[...], crossed[...])


def tile_kernel(flags_ref, *refs):
    left, (have, other), (give_ref, keep_ref) = refs[:6], refs[6:8], refs[8:]
    same = flags_ref[1] == 1
    give = jnp.where(same, other[...], have[...])
    keep = jnp.where(same, have[...], other[...])
    right = halves(jnp.concatenate([give, keep], axis=1))
    for c in range(3):
        rows = slice(c * CHUNK, (c + 1) * CHUNK)
        for e in range(4):
            tile = product((left[2 * c][e], left[2 * c + 1][e]), right)
            give_ref[e, rows] = tile[:, :CHUNK]
            keep_ref[e, rows] = tile[:, CHUNK:]


def add_kernel(here_ref, one_ref, two_ref, *outs):
    for d, out in enumerate(outs):
        x = (here_ref[0] + d) % 4
        out[...] = one_ref[x] + two_ref[x]


def last_kernel(one, two, a, b, c, d, out):
    out[:, :CHUNK] = one[...]
    out[:, CHUNK : 2 * CHUNK] = two[...]
    out[:, 2 * CHUNK :] = (a[...] + b[...]) + (c[...] + d[...])


def swapped(value, axis):
    return lax.ppermute(value, axis, [(0, 1), (1, 0)])


def shifted(value, axis, distance):
    size = lax.axis_size(axis)
    return lax.ppermute(value, axis, [(i, (i + distance) % size) for i in range(size)])


def tie(value, *others):
    return lax.optimization_barrier((value,) + others)[0]


def along(value, moves):
    pairs = [(z * 4 + y, to_z * 4 + to_y) for (z, y), (to_z, to_y) in moves.items()]
    return lax.ppermute(value, ("zl", "y"), pairs)


def crossing(value):
    moves = {}
    for y in range(4):
        if y % 2 == 0:
            moves |= {(0, y): (3, y), (2, y): (1, y ^ 1)}
        else:
            moves |= {(3, y): (0, y), (1, y): (2, y ^ 1)}
    return along(value, moves)


class Order:
    def __init__(self):
        self.last = None

    def __call__(self, kernel, *operands):
        if self.last is not None:
            operands = lax.optimization_barrier(operands + (self.last,))[:-1]
        result = kernel(*operands)
        self.last = result[0] if isinstance(result, (list, tuple)) else result
        return result

    def after(self, value):
        self.last = lax.optimization_barrier((self.last, value))[0]


def body(three_index, occupied):
    rows = three_index.shape[1]
    aux, x, zl, zh, y = (lax.axis_index(a) for a in ("aux", "x", "zl", "zh", "y"))
    home = (zl // 2) == (y % 2)
    same = (zl + zl // 2 + y) % 2 == aux
    scalar = lambda *v: jnp.stack([jnp.asarray(a, jnp.int32) for a in v])
    x_here, y_here = scalar(x), scalar(y)
    pick = scalar(2 * zh + y // 2)
    flags = scalar(home, same)

    coeff = occupied.T
    share = coeff.shape[0] // 2
    sum_call = call(sum_kernel, f32(share, CHUNK), "vvvv")
    piece_call = call(piece_kernel, f32(4, PADDED, CHUNK), "vv")
    left_call = call(
        left_kernel,
        [bf16(4, CHUNK, DEPTH)] * 2 + [f32(DEPTH, CHUNK)],
        "ssvvvv",
        [pltpu.VMEM((4, 4, PADDED, CHUNK), jnp.float32)],
    )
    have_call = call(have_kernel, f32(DEPTH, CHUNK), "svv")
    tile_call = call(tile_kernel, [f32(4, rows, CHUNK)] * 2, "s" + "v" * 8)
    add_call = call(add_kernel, [f32(rows, CHUNK)] * 4, "svv")
    out_call = call(sum_kernel, f32(rows, CHUNK), "vvvv")
    last_call = call(last_kernel, f32(rows, 3 * CHUNK), "v" * 6)

    order = Order()
    first = order(functools.partial(half_call, 0, 1), y_here, three_index, coeff)
    rest = order(functools.partial(half_call, 1, 2), y_here, three_index, coeff)
    sends = [first, rest[:4], rest[4:]]

    def send_y(c):
        own, one, two, three = sends[c]
        if c == 2:
            one, two, three = lax.optimization_barrier((one, two, three, sums[0][0]))[:3]
        return own, shifted(two, "y", 2), shifted(one, "y", 1), shifted(three, "y", 3)

    def sum_y(parts):
        total = order(sum_call, *parts)
        return total, swapped(total, "zh")

    def over_x(total, other):
        return lax.all_to_all(order(piece_call, total, other), "x", 0, 0, tiled=True)

    def over_y(block):
        return [block] + [shifted(block, "y", d) for d in (1, 2, 3)]

    def left_of(blocks):
        high, low, mine = order(left_call, y_here, pick, *blocks)
        lefts.extend([high, low])
        return mine, crossing(mine)

    def pair_of(mine, crossed):
        have = order(have_call, flags, mine, crossed)
        return have, lax.ppermute(have, "zl", [(0, 1), (1, 0), (2, 3), (3, 2)])

    def tile_of(pair):
        give, keep = order(tile_call, flags, *lefts, *pair)
        return keep, swapped(give, "aux")

    def over_x_sum(keep, given):
        own, one, two, three = order(add_call, x_here, keep, given)
        return [own, shifted(two, "x", 2), shifted(one, "x", 1), shifted(three, "x", 3)]

    sums, lefts = [], []
    sums.append(sum_y(send_y(0)))
    sums.append(sum_y(send_y(1)))
    parts2 = send_y(2)
    order.after(parts2[1])
    block0 = over_x(*sums[0])
    sums.append(sum_y(parts2))
    block1 = over_x(*sums[1])
    blocks0 = over_y(block0)
    blocks1 = over_y(block1)
    blocks2 = over_y(over_x(*sums[2]))
    half0 = left_of(blocks0)
    half1 = left_of(blocks1)
    pair0 = pair_of(*half0)
    half2 = left_of(blocks2)
    pair1 = pair_of(*half1)
    tile0 = tile_of(pair0)
    tile1 = tile_of(pair1)
    pair2 = pair_of(*half2)
    out0 = over_x_sum(*tile0)
    out1 = over_x_sum(*tile1)
    tile2 = tile_of(pair2)
    out0 = order(out_call, *out0)
    out2 = over_x_sum(*tile2)
    out1 = order(out_call, *out1)
    return order(last_call, out0, out1, *out2)


def solution(mesh):
    fine = Mesh(mesh.devices.reshape(2, 4, 4, 2, 4), ("aux", "x", "zl", "zh", "y"))
    in_specs = (P("aux", ("x", "zl"), ("zh", "y")), P(("zh", "y"), None))
    out_specs = P(("x", "zl"), ("zh", "y", "aux"))
    return jax.shard_map(body, mesh=fine, in_specs=in_specs, out_specs=out_specs, check_vma=False)
```

```python
import functools

import jax
import jax.numpy as jnp
from jax import lax
from jax.experimental import pallas as pl
from jax.experimental.pallas import tpu as pltpu
from jax.sharding import Mesh, PartitionSpec as P

CHUNK = 128
SPLIT = (104, 96, 104, 96)
PADDED = 104
DEPTH = 4 * PADDED
VMEM_LIMIT = 24 * 1024 * 1024
HALF_LIMIT = 60 * 1024 * 1024
COST = pl.CostEstimate(flops=int(12e9), bytes_accessed=int(44e6), transcendentals=0)


def halves(value):
    high = value.astype(jnp.bfloat16)
    low = (value - high.astype(jnp.float32)).astype(jnp.bfloat16)
    return high, low


def product(left, right, contract=(1, 0)):
    (lh, ll), (rh, rl) = left, right
    dims = (((contract[0],), (contract[1],)), ((), ()))
    dot = functools.partial(lax.dot_general, dimension_numbers=dims, preferred_element_type=jnp.float32)
    return dot(lh, rh) + (dot(lh, rl) + dot(ll, rh))


def call(kernel, out_shape, spaces, scratch=()):
    vmem = pl.BlockSpec(memory_space=pltpu.VMEM)
    smem = pl.BlockSpec(memory_space=pltpu.SMEM)
    return pl.pallas_call(
        kernel,
        out_shape=out_shape,
        in_specs=[smem if s == "s" else vmem for s in spaces],
        out_specs=jax.tree.map(lambda _: vmem, out_shape),
        scratch_shapes=scratch,
        cost_estimate=COST,
        compiler_params=pltpu.CompilerParams(vmem_limit_bytes=VMEM_LIMIT),
    )


def f32(*shape):
    return jax.ShapeDtypeStruct(shape, jnp.float32)


def bf16(*shape):
    return jax.ShapeDtypeStruct(shape, jnp.bfloat16)


def half_kernel(count, here_ref, coeff_ref, *refs):
    blocks, outs, pieces = refs[:count], refs[count:-1], refs[-1]
    part = pl.program_id(0)
    coeff = halves(coeff_ref[...])
    for c, block in enumerate(blocks):
        for p in range(2):
            pieces[c, 2 * p + part] = product(coeff, halves(block[p]), (1, 1))

    @pl.when(part == 1)
    def _():
        for c in range(count):
            for d in range(4):
                outs[4 * c + d][...] = pieces[c, (here_ref[0] + d) % 4]


def half_call(first, count, here, three_index, coeff):
    size, cols = coeff.shape[0] // 2, coeff.shape[1]
    blocks = [pl.BlockSpec((2, CHUNK, cols), lambda i, c=c: (0, c, 0)) for c in range(first, first + count)]
    return pl.pallas_call(
        functools.partial(half_kernel, count),
        out_shape=[f32(size, CHUNK)] * (4 * count),
        grid=(2,),
        in_specs=[pl.BlockSpec(memory_space=pltpu.SMEM), pl.BlockSpec((size, cols), lambda i: (i, 0))] + blocks,
        out_specs=[pl.BlockSpec((size, CHUNK), lambda i: (0, 0))] * (4 * count),
        scratch_shapes=[pltpu.VMEM((count, 4, size, CHUNK), jnp.float32)],
        cost_estimate=COST,
        compiler_params=pltpu.CompilerParams(vmem_limit_bytes=HALF_LIMIT if first == 0 else VMEM_LIMIT),
    )(here, coeff, *[three_index] * count)


def sum_kernel(a, b, c, d, out):
    out[...] = (a[...] + b[...]) + (c[...] + d[...])


def piece_kernel(one_ref, two_ref, out):
    at = 0
    for i, size in enumerate(SPLIT):
        out[i, :size] = one_ref[at : at + size] + two_ref[at : at + size]
        if size < PADDED:
            out[i, size:] = jnp.zeros((PADDED - size, CHUNK), jnp.float32)
        at += size


def left_kernel(here_ref, pick_ref, a, b, c, d, high_ref, low_ref, mine_ref, held):
    here = here_ref[0]
    for i, ref in enumerate((a, b, c, d)):
        slot = (here - i + 4) % 4
        for e in range(4):
            held[e, slot] = ref[e]
    for e in range(4):
        high, low = halves(held[e].reshape(DEPTH, CHUNK).T)
        high_ref[e] = high
        low_ref[e] = low
    mine_ref[...] = held[pick_ref[0]].reshape(DEPTH, CHUNK)


def have_kernel(flags_ref, mine, crossed, out):
    out[...] = jnp.where(flags_ref[0] == 1, mine[...], crossed[...])


def tile_kernel(flags_ref, *refs):
    left, (have, other), (give_ref, keep_ref) = refs[:6], refs[6:8], refs[8:]
    same = flags_ref[1] == 1
    give = jnp.where(same, other[...], have[...])
    keep = jnp.where(same, have[...], other[...])
    right = halves(jnp.concatenate([give, keep], axis=1))
    for c in range(3):
        rows = slice(c * CHUNK, (c + 1) * CHUNK)
        for e in range(4):
            tile = product((left[2 * c][e], left[2 * c + 1][e]), right)
            give_ref[e, rows] = tile[:, :CHUNK]
            keep_ref[e, rows] = tile[:, CHUNK:]


def add_kernel(here_ref, one_ref, two_ref, *outs):
    for d, out in enumerate(outs):
        x = (here_ref[0] + d) % 4
        out[...] = one_ref[x] + two_ref[x]


def last_kernel(one, two, a, b, c, d, out):
    out[:, :CHUNK] = one[...]
    out[:, CHUNK : 2 * CHUNK] = two[...]
    out[:, 2 * CHUNK :] = (a[...] + b[...]) + (c[...] + d[...])


def swapped(value, axis):
    return lax.ppermute(value, axis, [(0, 1), (1, 0)])


def shifted(value, axis, distance):
    size = lax.axis_size(axis)
    return lax.ppermute(value, axis, [(i, (i + distance) % size) for i in range(size)])


def tie(value, *others):
    return lax.optimization_barrier((value,) + others)[0]


def along(value, moves):
    pairs = [(z * 4 + y, to_z * 4 + to_y) for (z, y), (to_z, to_y) in moves.items()]
    return lax.ppermute(value, ("zl", "y"), pairs)


def crossing(value):
    moves = {}
    for y in range(4):
        if y % 2 == 0:
            moves |= {(0, y): (3, y), (2, y): (1, y ^ 1)}
        else:
            moves |= {(3, y): (0, y), (1, y): (2, y ^ 1)}
    return along(value, moves)


class Order:
    def __init__(self):
        self.last = None

    def __call__(self, kernel, *operands):
        if self.last is not None:
            operands = lax.optimization_barrier(operands + (self.last,))[:-1]
        result = kernel(*operands)
        self.last = result[0] if isinstance(result, (list, tuple)) else result
        return result

    def after(self, value):
        self.last = lax.optimization_barrier((self.last, value))[0]


def body(three_index, occupied):
    rows = three_index.shape[1]
    aux, x, zl, zh, y = (lax.axis_index(a) for a in ("aux", "x", "zl", "zh", "y"))
    home = (zl // 2) == (y % 2)
    same = (zl + zl // 2 + y) % 2 == aux
    scalar = lambda *v: jnp.stack([jnp.asarray(a, jnp.int32) for a in v])
    x_here, y_here = scalar(x), scalar(y)
    pick = scalar(2 * zh + y // 2)
    flags = scalar(home, same)

    coeff = occupied.T
    share = coeff.shape[0] // 2
    sum_call = call(sum_kernel, f32(share, CHUNK), "vvvv")
    piece_call = call(piece_kernel, f32(4, PADDED, CHUNK), "vv")
    left_call = call(
        left_kernel,
        [bf16(4, CHUNK, DEPTH)] * 2 + [f32(DEPTH, CHUNK)],
        "ssvvvv",
        [pltpu.VMEM((4, 4, PADDED, CHUNK), jnp.float32)],
    )
    have_call = call(have_kernel, f32(DEPTH, CHUNK), "svv")
    tile_call = call(tile_kernel, [f32(4, rows, CHUNK)] * 2, "s" + "v" * 8)
    add_call = call(add_kernel, [f32(rows, CHUNK)] * 4, "svv")
    out_call = call(sum_kernel, f32(rows, CHUNK), "vvvv")
    last_call = call(last_kernel, f32(rows, 3 * CHUNK), "v" * 6)

    order = Order()
    first = order(functools.partial(half_call, 0, 1), y_here, three_index, coeff)
    rest = order(functools.partial(half_call, 1, 2), y_here, three_index, coeff)
    sends = [first, rest[:4], rest[4:]]

    def send_y(c):
        own, one, two, three = sends[c]
        if c == 2:
            one, two, three = lax.optimization_barrier((one, two, three, sums[0][0]))[:3]
        return own, shifted(two, "y", 2), shifted(one, "y", 1), shifted(three, "y", 3)

    def sum_y(parts):
        total = order(sum_call, *parts)
        return total, swapped(total, "zh")

    def over_x(total, other):
        return lax.all_to_all(order(piece_call, total, other), "x", 0, 0, tiled=True)

    def over_y(block):
        return [block] + [shifted(block, "y", d) for d in (1, 2, 3)]

    def left_of(blocks):
        high, low, mine = order(left_call, y_here, pick, *blocks)
        lefts.extend([high, low])
        return mine, crossing(mine)

    def pair_of(mine, crossed):
        have = order(have_call, flags, mine, crossed)
        return have, lax.ppermute(have, "zl", [(0, 1), (1, 0), (2, 3), (3, 2)])

    def tile_of(pair):
        give, keep = order(tile_call, flags, *lefts, *pair)
        return keep, swapped(give, "aux")

    def over_x_sum(keep, given):
        own, one, two, three = order(add_call, x_here, keep, given)
        return [own, shifted(two, "x", 2), shifted(one, "x", 1), shifted(three, "x", 3)]

    sums, lefts = [], []
    sums.append(sum_y(send_y(0)))
    sums.append(sum_y(send_y(1)))
    parts2 = send_y(2)
    order.after(parts2[1])
    block0 = over_x(*sums[0])
    sums.append(sum_y(parts2))
    block1 = over_x(*sums[1])
    blocks0 = over_y(block0)
    blocks1 = over_y(block1)
    blocks2 = over_y(over_x(*sums[2]))
    half0 = left_of(blocks0)
    half1 = left_of(blocks1)
    pair0 = pair_of(*half0)
    half2 = left_of(blocks2)
    pair1 = pair_of(*half1)
    tile0 = tile_of(pair0)
    tile1 = tile_of(pair1)
    out0 = over_x_sum(*tile0)
    pair2 = pair_of(*half2)
    out1 = over_x_sum(*tile1)
    tile2 = tile_of(pair2)
    out0 = order(out_call, *out0)
    out2 = over_x_sum(*tile2)
    out1 = order(out_call, *out1)
    return order(last_call, out0, out1, *out2)


def solution(mesh):
    fine = Mesh(mesh.devices.reshape(2, 4, 4, 2, 4), ("aux", "x", "zl", "zh", "y"))
    in_specs = (P("aux", ("x", "zl"), ("zh", "y")), P(("zh", "y"), None))
    out_specs = P(("x", "zl"), ("zh", "y", "aux"))
    return jax.shard_map(body, mesh=fine, in_specs=in_specs, out_specs=out_specs, check_vma=False)
```

```python
import functools

import jax
import jax.numpy as jnp
from jax import lax
from jax.experimental import pallas as pl
from jax.experimental.pallas import tpu as pltpu
from jax.sharding import Mesh, PartitionSpec as P

CHUNK = 128
SPLIT = (104, 96, 104, 96)
PADDED = 104
DEPTH = 4 * PADDED
VMEM_LIMIT = 24 * 1024 * 1024
HALF_LIMIT = 60 * 1024 * 1024
COST = pl.CostEstimate(flops=int(12e9), bytes_accessed=int(44e6), transcendentals=0)


def halves(value):
    high = value.astype(jnp.bfloat16)
    low = (value - high.astype(jnp.float32)).astype(jnp.bfloat16)
    return high, low


def product(left, right, contract=(1, 0)):
    (lh, ll), (rh, rl) = left, right
    dims = (((contract[0],), (contract[1],)), ((), ()))
    dot = functools.partial(lax.dot_general, dimension_numbers=dims, preferred_element_type=jnp.float32)
    return dot(lh, rh) + (dot(lh, rl) + dot(ll, rh))


def call(kernel, out_shape, spaces, scratch=()):
    vmem = pl.BlockSpec(memory_space=pltpu.VMEM)
    smem = pl.BlockSpec(memory_space=pltpu.SMEM)
    return pl.pallas_call(
        kernel,
        out_shape=out_shape,
        in_specs=[smem if s == "s" else vmem for s in spaces],
        out_specs=jax.tree.map(lambda _: vmem, out_shape),
        scratch_shapes=scratch,
        cost_estimate=COST,
        compiler_params=pltpu.CompilerParams(vmem_limit_bytes=VMEM_LIMIT),
    )


def f32(*shape):
    return jax.ShapeDtypeStruct(shape, jnp.float32)


def bf16(*shape):
    return jax.ShapeDtypeStruct(shape, jnp.bfloat16)


def half_kernel(count, here_ref, coeff_ref, *refs):
    blocks, outs, pieces = refs[:count], refs[count:-1], refs[-1]
    part = pl.program_id(0)
    coeff = halves(coeff_ref[...])
    for c, block in enumerate(blocks):
        for p in range(2):
            pieces[c, 2 * p + part] = product(coeff, halves(block[p]), (1, 1))

    @pl.when(part == 1)
    def _():
        for c in range(count):
            for d in range(4):
                outs[4 * c + d][...] = pieces[c, (here_ref[0] + d) % 4]


def half_call(first, count, here, three_index, coeff):
    size, cols = coeff.shape[0] // 2, coeff.shape[1]
    blocks = [pl.BlockSpec((2, CHUNK, cols), lambda i, c=c: (0, c, 0)) for c in range(first, first + count)]
    return pl.pallas_call(
        functools.partial(half_kernel, count),
        out_shape=[f32(size, CHUNK)] * (4 * count),
        grid=(2,),
        in_specs=[pl.BlockSpec(memory_space=pltpu.SMEM), pl.BlockSpec((size, cols), lambda i: (i, 0))] + blocks,
        out_specs=[pl.BlockSpec((size, CHUNK), lambda i: (0, 0))] * (4 * count),
        scratch_shapes=[pltpu.VMEM((count, 4, size, CHUNK), jnp.float32)],
        cost_estimate=COST,
        compiler_params=pltpu.CompilerParams(vmem_limit_bytes=HALF_LIMIT if first == 0 else VMEM_LIMIT),
    )(here, coeff, *[three_index] * count)


def sum_kernel(a, b, c, d, out):
    out[...] = (a[...] + b[...]) + (c[...] + d[...])


def piece_kernel(one_ref, two_ref, out):
    at = 0
    for i, size in enumerate(SPLIT):
        out[i, :size] = one_ref[at : at + size] + two_ref[at : at + size]
        if size < PADDED:
            out[i, size:] = jnp.zeros((PADDED - size, CHUNK), jnp.float32)
        at += size


def left_kernel(here_ref, pick_ref, a, b, c, d, high_ref, low_ref, mine_ref, held):
    here = here_ref[0]
    for i, ref in enumerate((a, b, c, d)):
        slot = (here - i + 4) % 4
        for e in range(4):
            held[e, slot] = ref[e]
    for e in range(4):
        high, low = halves(held[e].reshape(DEPTH, CHUNK).T)
        high_ref[e] = high
        low_ref[e] = low
    mine_ref[...] = held[pick_ref[0]].reshape(DEPTH, CHUNK)


def have_kernel(flags_ref, mine, crossed, out):
    out[...] = jnp.where(flags_ref[0] == 1, mine[...], crossed[...])


def tile_kernel(flags_ref, *refs):
    left, (have, other), (give_ref, keep_ref) = refs[:6], refs[6:8], refs[8:]
    same = flags_ref[1] == 1
    give = jnp.where(same, other[...], have[...])
    keep = jnp.where(same, have[...], other[...])
    right = halves(jnp.concatenate([give, keep], axis=1))
    for c in range(3):
        rows = slice(c * CHUNK, (c + 1) * CHUNK)
        for e in range(4):
            tile = product((left[2 * c][e], left[2 * c + 1][e]), right)
            give_ref[e, rows] = tile[:, :CHUNK]
            keep_ref[e, rows] = tile[:, CHUNK:]


def add_kernel(here_ref, one_ref, two_ref, *outs):
    for d, out in enumerate(outs):
        x = (here_ref[0] + d) % 4
        out[...] = one_ref[x] + two_ref[x]


def last_kernel(one, two, a, b, c, d, out):
    out[:, :CHUNK] = one[...]
    out[:, CHUNK : 2 * CHUNK] = two[...]
    out[:, 2 * CHUNK :] = (a[...] + b[...]) + (c[...] + d[...])


def swapped(value, axis):
    return lax.ppermute(value, axis, [(0, 1), (1, 0)])


def shifted(value, axis, distance):
    size = lax.axis_size(axis)
    return lax.ppermute(value, axis, [(i, (i + distance) % size) for i in range(size)])


def tie(value, *others):
    return lax.optimization_barrier((value,) + others)[0]


def along(value, moves):
    pairs = [(z * 4 + y, to_z * 4 + to_y) for (z, y), (to_z, to_y) in moves.items()]
    return lax.ppermute(value, ("zl", "y"), pairs)


def crossing(value):
    moves = {}
    for y in range(4):
        if y % 2 == 0:
            moves |= {(0, y): (3, y), (2, y): (1, y ^ 1)}
        else:
            moves |= {(3, y): (0, y), (1, y): (2, y ^ 1)}
    return along(value, moves)


class Order:
    def __init__(self):
        self.last = None

    def __call__(self, kernel, *operands):
        if self.last is not None:
            operands = lax.optimization_barrier(operands + (self.last,))[:-1]
        result = kernel(*operands)
        self.last = result[0] if isinstance(result, (list, tuple)) else result
        return result

    def after(self, value):
        self.last = lax.optimization_barrier((self.last, value))[0]


def body(three_index, occupied):
    rows = three_index.shape[1]
    aux, x, zl, zh, y = (lax.axis_index(a) for a in ("aux", "x", "zl", "zh", "y"))
    home = (zl // 2) == (y % 2)
    same = (zl + zl // 2 + y) % 2 == aux
    scalar = lambda *v: jnp.stack([jnp.asarray(a, jnp.int32) for a in v])
    x_here, y_here = scalar(x), scalar(y)
    pick = scalar(2 * zh + y // 2)
    flags = scalar(home, same)

    coeff = occupied.T
    share = coeff.shape[0] // 2
    sum_call = call(sum_kernel, f32(share, CHUNK), "vvvv")
    piece_call = call(piece_kernel, f32(4, PADDED, CHUNK), "vv")
    left_call = call(
        left_kernel,
        [bf16(4, CHUNK, DEPTH)] * 2 + [f32(DEPTH, CHUNK)],
        "ssvvvv",
        [pltpu.VMEM((4, 4, PADDED, CHUNK), jnp.float32)],
    )
    have_call = call(have_kernel, f32(DEPTH, CHUNK), "svv")
    tile_call = call(tile_kernel, [f32(4, rows, CHUNK)] * 2, "s" + "v" * 8)
    add_call = call(add_kernel, [f32(rows, CHUNK)] * 4, "svv")
    out_call = call(sum_kernel, f32(rows, CHUNK), "vvvv")
    last_call = call(last_kernel, f32(rows, 3 * CHUNK), "v" * 6)

    order = Order()
    first = order(functools.partial(half_call, 0, 1), y_here, three_index, coeff)
    rest = order(functools.partial(half_call, 1, 2), y_here, three_index, coeff)
    sends = [first, rest[:4], rest[4:]]

    def send_y(c):
        own, one, two, three = sends[c]
        if c == 2:
            one, two, three = lax.optimization_barrier((one, two, three, sums[0][0]))[:3]
        return own, shifted(two, "y", 2), shifted(one, "y", 1), shifted(three, "y", 3)

    def sum_y(parts):
        total = order(sum_call, *parts)
        return total, swapped(total, "zh")

    def over_x(total, other):
        return lax.all_to_all(order(piece_call, total, other), "x", 0, 0, tiled=True)

    def over_y(block):
        return [block] + [shifted(block, "y", d) for d in (1, 2, 3)]

    def left_of(blocks):
        high, low, mine = order(left_call, y_here, pick, *blocks)
        lefts.extend([high, low])
        return mine, crossing(mine)

    def pair_of(mine, crossed):
        have = order(have_call, flags, mine, crossed)
        return have, lax.ppermute(have, "zl", [(0, 1), (1, 0), (2, 3), (3, 2)])

    def tile_of(pair):
        give, keep = order(tile_call, flags, *lefts, *pair)
        return keep, swapped(give, "aux")

    def over_x_sum(keep, given):
        own, one, two, three = order(add_call, x_here, keep, given)
        return [own, shifted(two, "x", 2), shifted(one, "x", 1), shifted(three, "x", 3)]

    sums, lefts = [], []
    sums.append(sum_y(send_y(0)))
    sums.append(sum_y(send_y(1)))
    parts2 = send_y(2)
    order.after(parts2[1])
    block0 = over_x(*sums[0])
    sums.append(sum_y(parts2))
    block1 = over_x(*sums[1])
    blocks0 = over_y(block0)
    blocks1 = over_y(block1)
    blocks2 = over_y(over_x(*sums[2]))
    half0 = left_of(blocks0)
    half1 = left_of(blocks1)
    pair0 = pair_of(*half0)
    half2 = left_of(blocks2)
    pair1 = pair_of(*half1)
    tile0 = tile_of(pair0)
    tile1 = tile_of(pair1)
    pair2 = pair_of(*half2)
    out0 = over_x_sum(*tile0)
    tile2 = tile_of(pair2)
    out1 = over_x_sum(*tile1)
    out0 = order(out_call, *out0)
    out2 = over_x_sum(*tile2)
    out1 = order(out_call, *out1)
    return order(last_call, out0, out1, *out2)


def solution(mesh):
    fine = Mesh(mesh.devices.reshape(2, 4, 4, 2, 4), ("aux", "x", "zl", "zh", "y"))
    in_specs = (P("aux", ("x", "zl"), ("zh", "y")), P(("zh", "y"), None))
    out_specs = P(("x", "zl"), ("zh", "y", "aux"))
    return jax.shard_map(body, mesh=fine, in_specs=in_specs, out_specs=out_specs, check_vma=False)
```
